32 devices in a mesh: dp: 4 (over x, core), feat: 8 (over z, y).
Axes of the slice: x: 2, y: 2, z: 4, core: 2. Of those that a mesh axis runs over, the one named last changes fastest.
Arguments:
- tokens: bfloat16 [512, 16384], P('dp', 'feat'), may hold values from -6 to 6
- cotangent: bfloat16 [512, 16384], P('dp', 'feat'), may hold values from -6 to 6
- factor_in: bfloat16 [7, 128, 2, 128, 128], P(None, 'feat', None, 'dp'), may hold values from -0.375 to 0.375
- factor_out: bfloat16 [7, 128, 2, 128, 128], P(None, 'feat', None, 'dp'), may hold values from -0.375 to 0.375
Outputs:
- outputs: bfloat16 [512, 16384], P('dp', 'feat')
- token_grad: bfloat16 [512, 16384], P('dp', 'feat')
- factor_in_grad: float32 [7, 128, 2, 128, 128], P(None, 'feat', None, 'dp')
- factor_out_grad: float32 [7, 128, 2, 128, 128], P(None, 'feat', None, 'dp')
The draws below stay inside these ranges and needn't reach their ends.
All inputs are finite; a program needn't handle non-finite values.
Results may differ from the reference program's by a relative error of at most 0.035.
Values may be sent and summed in bfloat16 or wider, within the bound.
A program may use at most 128 MiB of HBM per device.

```python
import jax
import jax.numpy as jnp
from jax import lax

B = 128
NB = 128
LEVELS = 7
TOK_DEV = 128
W = 16384
TOKENS = 512
N_DP = 4


def steps_of(key, dims, cuts, smallest, largest):
    factor_of = 1.0
    for axis_at, parts in cuts:
        heights = jax.random.uniform(jax.random.fold_in(jax.random.fold_in(key, 6), axis_at), (parts,), jnp.float32, smallest / len(cuts), largest / len(cuts))
        factor_of = factor_of * jnp.repeat(jnp.exp(heights), dims[axis_at] // parts).reshape((-1,) + (1,) * (len(dims) - 1 - axis_at))
    return factor_of


def gaussian(own_key, extent, deviation, reach, cuts=(), kind=jnp.bfloat16):
    drawn = deviation * jax.random.normal(own_key, extent, jnp.float32)
    if cuts:
        drawn = drawn * steps_of(own_key, extent, cuts, -0.22, 0.18)
    return jnp.clip(drawn, -reach, reach).astype(kind)


def setup_inputs(seed: int = 0) -> dict:
    streams_of = jax.random.split(jax.random.key(seed), 5)
    tokens = gaussian(streams_of[0], (TOKENS, W), 1.0, 6.0, ((0, 4), (1, 8)))
    cotangent = gaussian(streams_of[1], (TOKENS, W), 1.0, 6.0, ((0, 4), (1, 8)))
    factor_in = gaussian(streams_of[2], (LEVELS, NB, 2, B, B), (2 * B) ** -0.5, 0.375, ((1, 8), (3, 4)))
    factor_out = gaussian(streams_of[3], (LEVELS, NB, 2, B, B), (2 * B) ** -0.5, 0.375, ((1, 8), (3, 4)))
    return dict(tokens=tokens, cotangent=cotangent, factor_in=factor_in, factor_out=factor_out)


def flip_blocks(values, bit_no):
    row_count, block_count, block_cols = values.shape
    span = 2 ** bit_no
    grouped = values.reshape(row_count, block_count // (2 * span), 2, span, block_cols)
    return jnp.flip(grouped, 2).reshape(row_count, block_count, block_cols)

def apply_level(values, partner, factor):
    own_term = jnp.einsum('tjr,jrc->tjc', values.astype(jnp.float32), factor[:, 0].astype(jnp.float32))
    other_term = jnp.einsum('tjr,jrc->tjc', partner.astype(jnp.float32), factor[:, 1].astype(jnp.float32))
    return own_term + other_term

def gelu_exact(pre_act):
    return 0.5 * pre_act * (1.0 + lax.erf(pre_act * 0.7071067811865476))

def gelu_slope(pre_act):
    return 0.5 * (1.0 + lax.erf(pre_act * 0.7071067811865476)) + pre_act * jnp.exp(-0.5 * pre_act * pre_act) * 0.3989422804014327

def group_sum(left, right, grad_scale):
    left_groups = left.astype(jnp.float32).reshape(N_DP, TOK_DEV, NB, B)
    right_groups = right.reshape(N_DP, TOK_DEV, NB, B)
    partial_sums = jnp.einsum('ntjr,ntjc->njrc', left_groups, right_groups) * grad_scale
    rounded = lax.optimization_barrier(partial_sums.astype(jnp.bfloat16))
    return lax.optimization_barrier(jnp.sum(rounded.astype(jnp.float32), 0))

def backward_map(grad_in, stored, factor, grad_scale):
    level_grads = []
    current = grad_in
    for layer_no in reversed(range(LEVELS)):
        values = stored[layer_no]
        partner = flip_blocks(values, layer_no)
        cur32 = current.astype(jnp.float32)
        d_self = group_sum(values, cur32, grad_scale)
        d_part = group_sum(partner, cur32, grad_scale)
        level_grads.append(jnp.stack([d_self, d_part], 1))
        outgoing = jnp.einsum('tjc,jrc->tjr', cur32, factor[layer_no, :, 1].astype(jnp.float32)).astype(jnp.bfloat16)
        incoming = flip_blocks(outgoing, layer_no)
        own_term = jnp.einsum('tjc,jrc->tjr', cur32, factor[layer_no, :, 0].astype(jnp.float32))
        current = (own_term + incoming.astype(jnp.float32)).astype(jnp.bfloat16)
    return (current, jnp.stack(level_grads[::-1], 0))

def reference(tokens, cotangent, factor_in, factor_out):
    grad_scale = 1.0 / jnp.sqrt(jnp.float32(TOKENS))
    current = tokens.reshape(TOKENS, NB, B)
    stored_in = []
    for layer_no in range(LEVELS):
        stored_in.append(current)
        summed = apply_level(current, flip_blocks(current, layer_no), factor_in[layer_no])
        if layer_no < LEVELS - 1:
            current = summed.astype(jnp.bfloat16)
    pre_gelu = summed
    current = gelu_exact(pre_gelu).astype(jnp.bfloat16)
    stored_out = []
    for layer_no in range(LEVELS):
        stored_out.append(current)
        current = apply_level(current, flip_blocks(current, layer_no), factor_out[layer_no]).astype(jnp.bfloat16)
    outputs = current.reshape(TOKENS, W)
    grad_mid, factor_out_grad = backward_map(cotangent.reshape(TOKENS, NB, B), stored_out, factor_out, grad_scale)
    grad_pre = (grad_mid.astype(jnp.float32) * gelu_slope(pre_gelu)).astype(jnp.bfloat16)
    token_grad, factor_in_grad = backward_map(grad_pre, stored_in, factor_in, grad_scale)
    return (outputs, token_grad.reshape(TOKENS, W), factor_in_grad, factor_out_grad)
```

```python
import functools
import math

import jax
import jax.numpy as jnp
from jax import lax
from jax.experimental import pallas as pl
from jax.experimental.pallas import tpu as pltpu
from jax.sharding import PartitionSpec as P


def partner_2(value, axis, stride):
    mask = 2**stride
    pairs = [(source, source ^ mask) for source in range(lax.axis_size(axis))]
    return lax.ppermute(value, axis, pairs)


def flip_blocks(values, bit_no):
    row_count, block_count, block_cols = values.shape
    span = 2**bit_no
    grouped = values.reshape(row_count, block_count // (2 * span), 2, span, block_cols)
    return jnp.flip(grouped, 2).reshape(row_count, block_count, block_cols)


def act_partner(values, bit_no, local_bits):
    if bit_no < local_bits:
        return flip_blocks(values, bit_no)
    return partner_2(values, "feat", bit_no - local_bits)


def grad_partner(values, bit_no, local_bits):
    if bit_no < local_bits:
        return flip_blocks(values, bit_no)
    return partner_2(values, "feat", bit_no - local_bits)


def gelu_exact(pre_act):
    return 0.5 * pre_act * (1.0 + lax.erf(pre_act * 0.7071067811865476))


def gelu_slope(pre_act):
    return (
        0.5 * (1.0 + lax.erf(pre_act * 0.7071067811865476))
        + pre_act * jnp.exp(-0.5 * pre_act * pre_act) * 0.3989422804014327
    )


def apply_level(values, partner, factor):
    own_term = jnp.einsum("tjr,jrc->tjc", values, factor[:, 0], preferred_element_type=jnp.float32)
    other_term = jnp.einsum(
        "tjr,jrc->tjc", partner, factor[:, 1], preferred_element_type=jnp.float32
    )
    return own_term + other_term


def gather_level(factor_shard):
    return lax.all_gather(factor_shard, "dp", axis=2, tiled=True)


def sum_level(level_grad):
    return lax.psum_scatter(
        level_grad.astype(jnp.bfloat16), "dp", scatter_dimension=2, tiled=True
    ).astype(jnp.float32)


def forward_map(current, factors, local_bits, last_plain):
    stored = []
    for layer_no in range(len(factors)):
        partner = act_partner(current, layer_no, local_bits)
        stored.append((current, partner))
        summed = apply_level(current, partner, factors[layer_no])
        if layer_no < len(factors) - 1 or not last_plain:
            current = summed.astype(jnp.bfloat16)
    return (summed, current, stored)


def backward_map(grad_in, stored, factors, local_bits, grad_scale):
    level_grads = [None] * len(factors)
    current = grad_in
    for layer_no in reversed(range(len(factors))):
        values, partner = stored[layer_no]
        factor = factors[layer_no]
        d_self = jnp.einsum("tjr,tjc->jrc", values, current, preferred_element_type=jnp.float32)
        d_part = jnp.einsum("tjr,tjc->jrc", partner, current, preferred_element_type=jnp.float32)
        level_grad = jnp.stack([d_self, d_part], 1) * grad_scale
        level_grads[layer_no] = sum_level(level_grad)
        outgoing = jnp.einsum(
            "tjc,jrc->tjr", current, factor[:, 1], preferred_element_type=jnp.float32
        ).astype(jnp.bfloat16)
        incoming = grad_partner(outgoing, layer_no, local_bits)
        own_term = jnp.einsum(
            "tjc,jrc->tjr", current, factor[:, 0], preferred_element_type=jnp.float32
        )
        current = (own_term + incoming.astype(jnp.float32)).astype(jnp.bfloat16)
    stacked = jnp.stack(level_grads, 0)
    return (current, stacked)


def on_device(tokens, cotangent, factor_in, factor_out):
    level_count = factor_in.shape[0]
    block_cols = factor_in.shape[4]
    local_blocks = factor_in.shape[1]
    local_bits = local_blocks.bit_length() - 1
    tok_rows = tokens.shape[0]
    grad_scale = 1.0 / math.sqrt(tok_rows * lax.axis_size("dp"))
    factors_first = [gather_level(factor_in[layer_no]) for layer_no in range(level_count)]
    factors_second = [gather_level(factor_out[layer_no]) for layer_no in range(level_count)]
    current = tokens.reshape(tok_rows, local_blocks, block_cols)
    pre_gelu, unused_last, stored_in = forward_map(current, factors_first, local_bits, True)
    hidden = gelu_exact(pre_gelu).astype(jnp.bfloat16)
    unused_sum, mapped, stored_out = forward_map(hidden, factors_second, local_bits, False)
    outputs = mapped.reshape(tok_rows, local_blocks * block_cols)
    grad_mid, factor_out_grad = backward_map(
        cotangent.reshape(tok_rows, local_blocks, block_cols),
        stored_out,
        factors_second,
        local_bits,
        grad_scale,
    )
    grad_pre = (grad_mid.astype(jnp.float32) * gelu_slope(pre_gelu)).astype(jnp.bfloat16)
    token_grad, factor_in_grad = backward_map(
        grad_pre, stored_in, factors_first, local_bits, grad_scale
    )
    return (
        outputs,
        token_grad.reshape(tok_rows, local_blocks * block_cols),
        factor_in_grad,
        factor_out_grad,
    )


def block_of(values, j, width):
    return values[:, j * width:(j + 1) * width]


def start_factor_copies(pieces, factor_buf, sems, levels):
    me = lax.axis_index("dp")
    rows = pieces[0].shape[3]
    copies = []
    for slot, level in enumerate(levels):
        row = []
        for k, piece in enumerate(pieces):
            at = pl.multiple_of((me ^ k) * rows, rows)
            copy = pltpu.make_async_copy(
                piece.at[level],
                factor_buf.at[slot, :, :, pl.ds(at, rows), :],
                sems.at[slot, k],
            )
            copy.start()
            row.append(copy)
        copies.append(row)
    return copies


def merged(factor_buf, slot, j):
    both = factor_buf[slot, j]
    return both.reshape(both.shape[0] * both.shape[1], both.shape[2])


def forward_kernel(levels, bits, partner_given, *refs):
    n = len(levels)
    values = refs[0]
    partner = refs[1] if partner_given else None
    base = 2 if partner_given else 1
    pieces = refs[base:base + 4]
    outs = refs[base + 4:base + 4 + n]
    factor_buf, sems = refs[base + 4 + n:]
    width = factor_buf.shape[3]
    count = factor_buf.shape[1]
    copies = start_factor_copies(pieces, factor_buf, sems, levels)
    for slot in range(n):
        for copy in copies[slot]:
            copy.wait()
        for j in range(count):
            if partner_given:
                other = block_of(partner, j, width)
            else:
                other = block_of(values, j ^ (1 << bits[slot]), width)
            pair = jnp.concatenate([block_of(values, j, width), other], axis=1)
            got = jnp.dot(pair, merged(factor_buf, slot, j), preferred_element_type=jnp.float32)
            outs[slot][:, j * width:(j + 1) * width] = got.astype(outs[slot].dtype)
        values = outs[slot]


def backward_kernel(levels, bits, remote, summed, *refs):
    n = len(levels)
    base = 2 if summed else 1
    pieces = refs[base:base + 4]
    n_out = (2 if remote else n) + (1 if summed else 0)
    outs = list(refs[base + 4:base + 4 + n_out])
    factor_buf, sems = refs[base + 4 + n_out:base + 6 + n_out]
    width = factor_buf.shape[3]
    count = factor_buf.shape[1]
    copies = start_factor_copies(pieces, factor_buf, sems, levels)
    current = refs[0]
    if summed:
        first = outs.pop(0)
        first[...] = (refs[0][...] + refs[1][...].astype(jnp.float32)).astype(first.dtype)
        current = first
    for slot in range(n):
        for copy in copies[slot]:
            copy.wait()

        def through(j):
            got = lax.dot_general(
                block_of(current, j, width),
                merged(factor_buf, slot, j),
                (((1,), (1,)), ((), ())),
                preferred_element_type=jnp.float32,
            )
            return got[:, :width], got[:, width:].astype(jnp.bfloat16)

        for j in range(count):
            if remote:
                own, other = through(j)
                outs[0][:, j * width:(j + 1) * width] = own
                outs[1][:, j * width:(j + 1) * width] = other
            else:
                p = j ^ (1 << bits[slot])
                if p < j:
                    continue
                own_j, other_j = through(j)
                own_p, other_p = through(p)
                dst = outs[slot]
                dst[:, j * width:(j + 1) * width] = (
                    own_j + other_p.astype(jnp.float32)
                ).astype(dst.dtype)
                dst[:, p * width:(p + 1) * width] = (
                    own_p + other_j.astype(jnp.float32)
                ).astype(dst.dtype)
        if not remote:
            current = outs[slot]


def grad_kernel(bits, remote, grad_scale, *refs):
    n = len(bits)
    values = refs[:n]
    partners = refs[n:2 * n] if remote else None
    base = 2 * n if remote else n
    grads = refs[base:base + n]
    keep, send = refs[base + n:]
    count = keep.shape[2]
    rows = keep.shape[4]
    width = keep.shape[5]
    me = lax.axis_index("dp")
    core = me % 2
    x_at = me // 2
    for slot in range(n):
        for j in range(count):
            if remote:
                other = block_of(partners[slot], j, width)
            else:
                other = block_of(values[slot], j ^ (1 << bits[slot]), width)
            pair = jnp.concatenate([block_of(values[slot], j, width), other], axis=1)
            got = lax.dot_general(
                pair,
                block_of(grads[slot], j, width),
                (((0,), (0,)), ((), ())),
                preferred_element_type=jnp.float32,
            ) * grad_scale
            for term in range(2):
                for x_to in range(2):
                    at = term * width + x_to * 2 * rows
                    low = got[at:at + rows]
                    high = got[at + rows:at + 2 * rows]
                    k_x = x_at ^ x_to
                    keep[k_x, slot, j, term] = jnp.where(core == 0, low, high).astype(keep.dtype)
                    send[k_x, slot, j, term] = jnp.where(core == 0, high, low).astype(send.dtype)


VMEM = pl.BlockSpec(memory_space=pltpu.VMEM)
ANY = pl.BlockSpec(memory_space=pl.ANY)
PARAMS = dict(compiler_params=pltpu.CompilerParams(vmem_limit_bytes=40 * 2**20))


def estimate(n_levels, tok_rows, count, width, moved):
    return pl.CostEstimate(
        flops=4 * n_levels * tok_rows * count * width * width,
        bytes_accessed=moved,
        transcendentals=0,
    )


def call_forward(values, partner, pieces, levels, bits, out_type=jnp.bfloat16):
    n = len(levels)
    _, count, two, rows, width = pieces[0].shape
    acts = [values] if partner is None else [values, partner]
    buf = (n, count, two, 4 * rows, width)
    return pl.pallas_call(
        functools.partial(forward_kernel, levels, bits, partner is not None),
        out_shape=[jax.ShapeDtypeStruct(values.shape, out_type)] * n,
        in_specs=[VMEM] * len(acts) + [ANY] * 4,
        out_specs=[VMEM] * n,
        scratch_shapes=[pltpu.VMEM(buf, jnp.bfloat16), pltpu.SemaphoreType.DMA((n, 4))],
        cost_estimate=estimate(n, values.shape[0], count, width, 2 * math.prod(buf) + 4 * n * values.size),
        **PARAMS,
    )(*acts, *pieces)


def call_backward(incoming, pieces, levels, bits, remote):
    n = len(levels)
    _, count, two, rows, width = pieces[0].shape
    buf = (n, count, two, 4 * rows, width)
    shape = incoming[0].shape
    low = jax.ShapeDtypeStruct(shape, jnp.bfloat16)
    outs = [low] if len(incoming) == 2 else []
    outs += [jax.ShapeDtypeStruct(shape, jnp.float32), low] if remote else [low] * n
    return pl.pallas_call(
        functools.partial(backward_kernel, levels, bits, remote, len(incoming) == 2),
        out_shape=outs,
        in_specs=[VMEM] * len(incoming) + [ANY] * 4,
        out_specs=[VMEM] * len(outs),
        scratch_shapes=[pltpu.VMEM(buf, jnp.bfloat16), pltpu.SemaphoreType.DMA((n, 4))],
        cost_estimate=estimate(n, shape[0], count, width, 2 * math.prod(buf) + 6 * n * math.prod(shape)),
        **PARAMS,
    )(*incoming, *pieces)


def call_grads(values, partners, grads, bits, rows, grad_scale):
    n = len(bits)
    tok_rows, features = values[0].shape
    width = 4 * rows
    count = features // width
    out = jax.ShapeDtypeStruct((2, n, count, 2, rows, width), jnp.bfloat16)
    acts = list(values) + list(partners or []) + list(grads)
    return pl.pallas_call(
        functools.partial(grad_kernel, bits, partners is not None, grad_scale),
        out_shape=[out, out],
        in_specs=[VMEM] * len(acts),
        out_specs=[VMEM] * 2,
        cost_estimate=estimate(n, tok_rows, count, width, 10 * n * values[0].size),
        **PARAMS,
    )(*acts)


def sum_pairs(keep, send):
    got = partner_dp(send, 1)
    across = (keep[1].astype(jnp.float32) + got[1].astype(jnp.float32)).astype(jnp.bfloat16)
    mine = keep[0].astype(jnp.float32) + got[0].astype(jnp.float32)
    return mine + partner_dp(across, 2).astype(jnp.float32)


def partner_dp(value, mask):
    return lax.ppermute(value, "dp", [(k, k ^ mask) for k in range(lax.axis_size("dp"))])


def gather_pairs(shard):
    near = partner_dp(shard, 1)
    far = partner_dp(shard, 2)
    return [shard, near, far, partner_dp(far, 1)]


def on_device_pairs(tokens, cotangent, factor_in, factor_out):
    level_count, local_blocks, _, rows, width = factor_in.shape
    local_bits = local_blocks.bit_length() - 1
    grad_scale = 1.0 / math.sqrt(tokens.shape[0] * lax.axis_size("dp"))
    low = tuple(range(local_bits))
    high = tuple(range(local_bits, level_count))

    in_low = gather_pairs(factor_in[:local_bits])
    in_high = gather_pairs(factor_in[local_bits:])
    out_high = gather_pairs(factor_out[local_bits:])
    out_low = gather_pairs(factor_out[:local_bits])

    def over_feat(value, level):
        return partner_2(value, "feat", level - local_bits)

    def forward(values, pieces_low, pieces_high, last_type):
        stored = [values] + list(call_forward(values, None, pieces_low, low, low))
        partners = []
        for level in high:
            partner = over_feat(stored[level], level)
            partners.append(partner)
            out_type = last_type if level == level_count - 1 else jnp.bfloat16
            stored += call_forward(
                stored[level], partner, pieces_high, (level - local_bits,), (level,), out_type
            )
        return stored, partners

    def backward(grad, pieces_low, pieces_high):
        grads = [None] * level_count
        incoming = [grad]
        for level in reversed(high):
            *head, own, other = call_backward(
                incoming, pieces_high, (level - local_bits,), (level,), True
            )
            if level == level_count - 1:
                grads[level] = grad
            else:
                grads[level] = head[0]
            incoming = [own, over_feat(other, level)]
        down = tuple(reversed(low))
        got = call_backward(incoming, pieces_low, down, down, False)
        for place, level in enumerate(down):
            grads[level] = got[place]
        return got[-1], grads

    def level_sums(stored, partners, grads, group):
        remote = group[0] >= local_bits
        keep, send = call_grads(
            [stored[level] for level in group],
            [partners[level - local_bits] for level in group] if remote else None,
            [grads[level] for level in group],
            group,
            rows,
            grad_scale,
        )
        return sum_pairs(keep, send)

    stored_in, partners_in = forward(tokens, in_low, in_high, jnp.float32)
    grad_mid, grads_out = backward(cotangent, out_low, out_high)
    pre_gelu = stored_in[-1]
    hidden = gelu_exact(pre_gelu).astype(jnp.bfloat16)
    grad_pre = (grad_mid.astype(jnp.float32) * gelu_slope(pre_gelu)).astype(jnp.bfloat16)
    stored_out, partners_out = forward(hidden, out_low, out_high, jnp.bfloat16)
    token_grad, grads_in = backward(grad_pre, in_low, in_high)
    half = local_bits // 2
    groups = [low[:half], low[half:], high]
    sums_out = [level_sums(stored_out, partners_out, grads_out, group) for group in groups]
    sums_in = [level_sums(stored_in, partners_in, grads_in, group) for group in reversed(groups)]
    return (
        stored_out[-1],
        token_grad,
        jnp.concatenate(sums_in[::-1], 0),
        jnp.concatenate(sums_out, 0),
    )


def solution(mesh):
    placed = (
        P("dp", "feat"),
        P("dp", "feat"),
        P(None, "feat", None, "dp", None),
        P(None, "feat", None, "dp", None),
    )
    pairs = mesh.shape["dp"] == 4
    return jax.shard_map(
        on_device_pairs if pairs else on_device,
        mesh=mesh,
        in_specs=placed,
        out_specs=(
            P("dp", "feat"),
            P("dp", "feat"),
            P(None, "feat", None, "dp", None),
            P(None, "feat", None, "dp", None),
        ),
        check_vma=False,
    )
```

```python
import functools
import math

import jax
import jax.numpy as jnp
from jax import lax
from jax.experimental import pallas as pl
from jax.experimental.pallas import tpu as pltpu
from jax.sharding import PartitionSpec as P


def partner_2(value, axis, stride):
    mask = 2**stride
    pairs = [(source, source ^ mask) for source in range(lax.axis_size(axis))]
    return lax.ppermute(value, axis, pairs)


def flip_blocks(values, bit_no):
    row_count, block_count, block_cols = values.shape
    span = 2**bit_no
    grouped = values.reshape(row_count, block_count // (2 * span), 2, span, block_cols)
    return jnp.flip(grouped, 2).reshape(row_count, block_count, block_cols)


def act_partner(values, bit_no, local_bits):
    if bit_no < local_bits:
        return flip_blocks(values, bit_no)
    return partner_2(values, "feat", bit_no - local_bits)


def grad_partner(values, bit_no, local_bits):
    if bit_no < local_bits:
        return flip_blocks(values, bit_no)
    return partner_2(values, "feat", bit_no - local_bits)


def gelu_exact(pre_act):
    return 0.5 * pre_act * (1.0 + lax.erf(pre_act * 0.7071067811865476))


def gelu_slope(pre_act):
    return (
        0.5 * (1.0 + lax.erf(pre_act * 0.7071067811865476))
        + pre_act * jnp.exp(-0.5 * pre_act * pre_act) * 0.3989422804014327
    )


def apply_level(values, partner, factor):
    own_term = jnp.einsum("tjr,jrc->tjc", values, factor[:, 0], preferred_element_type=jnp.float32)
    other_term = jnp.einsum(
        "tjr,jrc->tjc", partner, factor[:, 1], preferred_element_type=jnp.float32
    )
    return own_term + other_term


def gather_level(factor_shard):
    return lax.all_gather(factor_shard, "dp", axis=2, tiled=True)


def sum_level(level_grad):
    return lax.psum_scatter(
        level_grad.astype(jnp.bfloat16), "dp", scatter_dimension=2, tiled=True
    ).astype(jnp.float32)


def forward_map(current, factors, local_bits, last_plain):
    stored = []
    for layer_no in range(len(factors)):
        partner = act_partner(current, layer_no, local_bits)
        stored.append((current, partner))
        summed = apply_level(current, partner, factors[layer_no])
        if layer_no < len(factors) - 1 or not last_plain:
            current = summed.astype(jnp.bfloat16)
    return (summed, current, stored)


def backward_map(grad_in, stored, factors, local_bits, grad_scale):
    level_grads = [None] * len(factors)
    current = grad_in
    for layer_no in reversed(range(len(factors))):
        values, partner = stored[layer_no]
        factor = factors[layer_no]
        d_self = jnp.einsum("tjr,tjc->jrc", values, current, preferred_element_type=jnp.float32)
        d_part = jnp.einsum("tjr,tjc->jrc", partner, current, preferred_element_type=jnp.float32)
        level_grad = jnp.stack([d_self, d_part], 1) * grad_scale
        level_grads[layer_no] = sum_level(level_grad)
        outgoing = jnp.einsum(
            "tjc,jrc->tjr", current, factor[:, 1], preferred_element_type=jnp.float32
        ).astype(jnp.bfloat16)
        incoming = grad_partner(outgoing, layer_no, local_bits)
        own_term = jnp.einsum(
            "tjc,jrc->tjr", current, factor[:, 0], preferred_element_type=jnp.float32
        )
        current = (own_term + incoming.astype(jnp.float32)).astype(jnp.bfloat16)
    stacked = jnp.stack(level_grads, 0)
    return (current, stacked)


def on_device(tokens, cotangent, factor_in, factor_out):
    level_count = factor_in.shape[0]
    block_cols = factor_in.shape[4]
    local_blocks = factor_in.shape[1]
    local_bits = local_blocks.bit_length() - 1
    tok_rows = tokens.shape[0]
    grad_scale = 1.0 / math.sqrt(tok_rows * lax.axis_size("dp"))
    factors_first = [gather_level(factor_in[layer_no]) for layer_no in range(level_count)]
    factors_second = [gather_level(factor_out[layer_no]) for layer_no in range(level_count)]
    current = tokens.reshape(tok_rows, local_blocks, block_cols)
    pre_gelu, unused_last, stored_in = forward_map(current, factors_first, local_bits, True)
    hidden = gelu_exact(pre_gelu).astype(jnp.bfloat16)
    unused_sum, mapped, stored_out = forward_map(hidden, factors_second, local_bits, False)
    outputs = mapped.reshape(tok_rows, local_blocks * block_cols)
    grad_mid, factor_out_grad = backward_map(
        cotangent.reshape(tok_rows, local_blocks, block_cols),
        stored_out,
        factors_second,
        local_bits,
        grad_scale,
    )
    grad_pre = (grad_mid.astype(jnp.float32) * gelu_slope(pre_gelu)).astype(jnp.bfloat16)
    token_grad, factor_in_grad = backward_map(
        grad_pre, stored_in, factors_first, local_bits, grad_scale
    )
    return (
        outputs,
        token_grad.reshape(tok_rows, local_blocks * block_cols),
        factor_in_grad,
        factor_out_grad,
    )


def block_of(values, j, width):
    return values[:, j * width:(j + 1) * width]


def start_factor_copies(pieces, factor_buf, sems, levels):
    me = lax.axis_index("dp")
    rows = pieces[0].shape[3]
    copies = []
    for slot, level in enumerate(levels):
        row = []
        for k, piece in enumerate(pieces):
            at = pl.multiple_of((me ^ k) * rows, rows)
            copy = pltpu.make_async_copy(
                piece.at[level],
                factor_buf.at[slot, :, :, pl.ds(at, rows), :],
                sems.at[slot, k],
            )
            copy.start()
            row.append(copy)
        copies.append(row)
    return copies


def merged(factor_buf, slot, j):
    both = factor_buf[slot, j]
    return both.reshape(both.shape[0] * both.shape[1], both.shape[2])


def forward_kernel(levels, bits, partner_given, *refs):
    n = len(levels)
    values = refs[0]
    partner = refs[1] if partner_given else None
    base = 2 if partner_given else 1
    pieces = refs[base:base + 4]
    outs = refs[base + 4:base + 4 + n]
    factor_buf, sems = refs[base + 4 + n:]
    width = factor_buf.shape[3]
    count = factor_buf.shape[1]
    copies = start_factor_copies(pieces, factor_buf, sems, levels)
    for slot in range(n):
        for copy in copies[slot]:
            copy.wait()
        for j in range(count):
            if partner_given:
                other = block_of(partner, j, width)
            else:
                other = block_of(values, j ^ (1 << bits[slot]), width)
            pair = jnp.concatenate([block_of(values, j, width), other], axis=1)
            got = jnp.dot(pair, merged(factor_buf, slot, j), preferred_element_type=jnp.float32)
            outs[slot][:, j * width:(j + 1) * width] = got.astype(outs[slot].dtype)
        values = outs[slot]


def backward_kernel(levels, bits, remote, summed, *refs):
    n = len(levels)
    base = 2 if summed else 1
    pieces = refs[base:base + 4]
    n_out = (2 if remote else n) + (1 if summed else 0)
    outs = list(refs[base + 4:base + 4 + n_out])
    factor_buf, sems = refs[base + 4 + n_out:base + 6 + n_out]
    width = factor_buf.shape[3]
    count = factor_buf.shape[1]
    copies = start_factor_copies(pieces, factor_buf, sems, levels)
    current = refs[0]
    if summed:
        first = outs.pop(0)
        first[...] = (refs[0][...] + refs[1][...].astype(jnp.float32)).astype(first.dtype)
        current = first
    for slot in range(n):
        for copy in copies[slot]:
            copy.wait()

        def through(j):
            got = lax.dot_general(
                block_of(current, j, width),
                merged(factor_buf, slot, j),
                (((1,), (1,)), ((), ())),
                preferred_element_type=jnp.float32,
            )
            return got[:, :width], got[:, width:].astype(jnp.bfloat16)

        for j in range(count):
            if remote:
                own, other = through(j)
                outs[0][:, j * width:(j + 1) * width] = own
                outs[1][:, j * width:(j + 1) * width] = other
            else:
                p = j ^ (1 << bits[slot])
                if p < j:
                    continue
                own_j, other_j = through(j)
                own_p, other_p = through(p)
                dst = outs[slot]
                dst[:, j * width:(j + 1) * width] = (
                    own_j + other_p.astype(jnp.float32)
                ).astype(dst.dtype)
                dst[:, p * width:(p + 1) * width] = (
                    own_p + other_j.astype(jnp.float32)
                ).astype(dst.dtype)
        if not remote:
            current = outs[slot]


def grad_kernel(bits, remote, grad_scale, *refs):
    n = len(bits)
    values = refs[:n]
    partners = refs[n:2 * n] if remote else None
    base = 2 * n if remote else n
    grads = refs[base:base + n]
    keep, send = refs[base + n:]
    count = keep.shape[2]
    rows = keep.shape[4]
    width = keep.shape[5]
    me = lax.axis_index("dp")
    core = me % 2
    x_at = me // 2
    for slot in range(n):
        for j in range(count):
            if remote:
                other = block_of(partners[slot], j, width)
            else:
                other = block_of(values[slot], j ^ (1 << bits[slot]), width)
            pair = jnp.concatenate([block_of(values[slot], j, width), other], axis=1)
            got = lax.dot_general(
                pair,
                block_of(grads[slot], j, width),
                (((0,), (0,)), ((), ())),
                preferred_element_type=jnp.float32,
            ) * grad_scale
            for term in range(2):
                for x_to in range(2):
                    at = term * width + x_to * 2 * rows
                    low = got[at:at + rows]
                    high = got[at + rows:at + 2 * rows]
                    k_x = x_at ^ x_to
                    keep[k_x, slot, j, term] = jnp.where(core == 0, low, high).astype(keep.dtype)
                    send[k_x, slot, j, term] = jnp.where(core == 0, high, low).astype(send.dtype)


VMEM = pl.BlockSpec(memory_space=pltpu.VMEM)
ANY = pl.BlockSpec(memory_space=pl.ANY)
PARAMS = dict(compiler_params=pltpu.CompilerParams(vmem_limit_bytes=40 * 2**20))


COST = pl.CostEstimate(flops=1, bytes_accessed=1, transcendentals=0)


def call_forward(values, partner, pieces, levels, bits, out_type=jnp.bfloat16):
    n = len(levels)
    _, count, two, rows, width = pieces[0].shape
    acts = [values] if partner is None else [values, partner]
    buf = (n, count, two, 4 * rows, width)
    return pl.pallas_call(
        functools.partial(forward_kernel, levels, bits, partner is not None),
        out_shape=[jax.ShapeDtypeStruct(values.shape, out_type)] * n,
        in_specs=[VMEM] * len(acts) + [ANY] * 4,
        out_specs=[VMEM] * n,
        scratch_shapes=[pltpu.VMEM(buf, jnp.bfloat16), pltpu.SemaphoreType.DMA((n, 4))],
        cost_estimate=COST,
        **PARAMS,
    )(*acts, *pieces)


def call_backward(incoming, pieces, levels, bits, remote):
    n = len(levels)
    _, count, two, rows, width = pieces[0].shape
    buf = (n, count, two, 4 * rows, width)
    shape = incoming[0].shape
    low = jax.ShapeDtypeStruct(shape, jnp.bfloat16)
    outs = [low] if len(incoming) == 2 else []
    outs += [jax.ShapeDtypeStruct(shape, jnp.float32), low] if remote else [low] * n
    return pl.pallas_call(
        functools.partial(backward_kernel, levels, bits, remote, len(incoming) == 2),
        out_shape=outs,
        in_specs=[VMEM] * len(incoming) + [ANY] * 4,
        out_specs=[VMEM] * len(outs),
        scratch_shapes=[pltpu.VMEM(buf, jnp.bfloat16), pltpu.SemaphoreType.DMA((n, 4))],
        cost_estimate=COST,
        **PARAMS,
    )(*incoming, *pieces)


def call_grads(values, partners, grads, bits, rows, grad_scale):
    n = len(bits)
    tok_rows, features = values[0].shape
    width = 4 * rows
    count = features // width
    out = jax.ShapeDtypeStruct((2, n, count, 2, rows, width), jnp.bfloat16)
    acts = list(values) + list(partners or []) + list(grads)
    return pl.pallas_call(
        functools.partial(grad_kernel, bits, partners is not None, grad_scale),
        out_shape=[out, out],
        in_specs=[VMEM] * len(acts),
        out_specs=[VMEM] * 2,
        cost_estimate=COST,
        **PARAMS,
    )(*acts)


def partner_dp(value, mask):
    return lax.ppermute(value, "dp", [(k, k ^ mask) for k in range(lax.axis_size("dp"))])


def after(value, earlier):
    return lax.optimization_barrier((value, earlier))[0]


def gather_pairs(shard, earlier=None):
    if earlier is not None:
        shard = after(shard, earlier)
    far = partner_dp(shard, 2)
    near = partner_dp(shard, 1)
    return [shard, near, far, partner_dp(far, 1)]


def on_device_pairs(tokens, cotangent, factor_in, factor_out):
    level_count, local_blocks, _, rows, width = factor_in.shape
    local_bits = local_blocks.bit_length() - 1
    top = level_count - 1
    grad_scale = 1.0 / math.sqrt(tokens.shape[0] * lax.axis_size("dp"))
    low = tuple(range(local_bits))
    down = tuple(reversed(low))
    high = tuple(range(local_bits, level_count))

    out_top = gather_pairs(factor_out[top:])
    in_low = gather_pairs(factor_in[:local_bits], out_top[2])
    gathered = {}

    def over_feat(value, level):
        return partner_2(value, "feat", level - local_bits)

    def in_place(level):
        return gathered["in_high"], level - local_bits

    def out_place(level):
        return (out_top, 0) if level == top else (gathered["out_high"], level - local_bits)

    def forward_low(values, pieces):
        return [values] + list(call_forward(values, None, pieces, low, low))

    def forward_high(value, partner, place, level, out_type=jnp.bfloat16):
        pieces, at = place(level)
        return call_forward(value, partner, pieces, (at,), (level,), out_type)[0]

    def backward_high(incoming, place, level):
        pieces, at = place(level)
        *head, own, other = call_backward(incoming, pieces, (at,), (level,), True)
        return (head[0] if head else incoming[0]), [own, over_feat(other, level)]

    def start_sums(values, partners, grads, group):
        remote = group[0] >= local_bits
        keep, send = call_grads(
            [values[level] for level in group],
            [partners[level] for level in group] if remote else None,
            [grads[level] for level in group],
            group,
            rows,
            grad_scale,
        )
        got = partner_dp(send, 1)
        across = (keep[1].astype(jnp.float32) + got[1].astype(jnp.float32)).astype(jnp.bfloat16)
        mine = keep[0].astype(jnp.float32) + got[0].astype(jnp.float32)
        return across, mine

    def cross(started):
        across, mine = started
        return partner_dp(across, 2), mine

    def end_sums(crossed):
        far, mine = crossed
        return mine + far.astype(jnp.float32)

    grads_out, partners_in = {}, {}
    incoming = [cotangent]
    grads_out[top], incoming = backward_high(incoming, out_place, top)
    gathered["in_high"] = gather_pairs(factor_in[local_bits:], (in_low[2], incoming[0]))
    acts_in = forward_low(tokens, in_low)
    gathered["out_high"] = gather_pairs(
        factor_out[local_bits:top], (gathered["in_high"][2], acts_in[-1], incoming[1])
    )
    for level in high:
        partners_in[level] = over_feat(acts_in[level], level)
        out_type = jnp.float32 if level == top else jnp.bfloat16
        acts_in.append(forward_high(acts_in[level], partners_in[level], in_place, level, out_type))
    out_low = gather_pairs(
        factor_out[:local_bits], (gathered["out_high"][2], acts_in[local_bits + 1])
    )
    for level in reversed(high[:-1]):
        grads_out[level], incoming = backward_high(incoming, out_place, level)
    got = call_backward(incoming, out_low, down, down, False)
    for place, level in enumerate(down):
        grads_out[level] = got[place]
    grad_mid, pre_gelu = got[-1], acts_in[-1]
    hidden = gelu_exact(pre_gelu).astype(jnp.bfloat16)
    grad_pre = (grad_mid.astype(jnp.float32) * gelu_slope(pre_gelu)).astype(jnp.bfloat16)

    grads_in, partners_out, sums_in, sums_out = {}, {}, {}, {}
    grads_in[top], incoming = backward_high([grad_pre], in_place, top)
    acts_out = forward_low(hidden, out_low)
    sums_in[top] = start_sums(acts_in, partners_in, grads_in, (top,))
    sums_out[0] = start_sums(acts_out, partners_out, grads_out, low)
    for level in high:
        partners_out[level] = over_feat(acts_out[level], level)
        if level == local_bits:
            partners_out[level] = after(partners_out[level], incoming[0])
        acts_out.append(forward_high(acts_out[level], partners_out[level], out_place, level))
    middle = high[:-1]
    for level in reversed(middle):
        if level == top - 1:
            incoming[0] = after(incoming[0], (sums_in[top][0], sums_out[0][0]))
        if level == local_bits:
            sums_in[top], sums_out[0] = cross(sums_in[top]), cross(sums_out[0])
            sums_out[local_bits] = start_sums(acts_out, partners_out, grads_out, middle)
            ready = (sums_in[top][0], sums_out[0][0], sums_out[local_bits][0], acts_out[top])
            incoming[0] = after(incoming[0], ready)
        grads_in[level], incoming = backward_high(incoming, in_place, level)
    sums_in[local_bits] = start_sums(acts_in, partners_in, grads_in, middle)
    sums_out[local_bits] = cross(sums_out[local_bits])
    ready = (sums_in[local_bits][0], sums_out[local_bits][0], partners_out[top])
    incoming[0] = after(incoming[0], ready)
    got = call_backward(incoming, in_low, down, down, False)
    for place, level in enumerate(down):
        grads_in[level] = got[place]
    sums_in[local_bits] = cross(sums_in[local_bits])
    sums_out[top] = cross(start_sums(acts_out, partners_out, grads_out, (top,)))
    across, mine = start_sums(acts_in, partners_in, grads_in, low)
    sums_in[0] = cross((after(across, sums_in[local_bits][0]), mine))
    return (
        acts_out[-1],
        got[-1],
        jnp.concatenate([end_sums(sums_in[level]) for level in sorted(sums_in)], 0),
        jnp.concatenate([end_sums(sums_out[level]) for level in sorted(sums_out)], 0),
    )


def solution(mesh):
    placed = (
        P("dp", "feat"),
        P("dp", "feat"),
        P(None, "feat", None, "dp", None),
        P(None, "feat", None, "dp", None),
    )
    pairs = mesh.shape["dp"] == 4
    return jax.shard_map(
        on_device_pairs if pairs else on_device,
        mesh=mesh,
        in_specs=placed,
        out_specs=(
            P("dp", "feat"),
            P("dp", "feat"),
            P(None, "feat", None, "dp", None),
            P(None, "feat", None, "dp", None),
        ),
        check_vma=False,
    )
```

```python
import functools
import math

import jax
import jax.numpy as jnp
from jax import lax
from jax.experimental import pallas as pl
from jax.experimental.pallas import tpu as pltpu
from jax.sharding import PartitionSpec as P


def partner_2(value, axis, stride):
    mask = 2**stride
    pairs = [(source, source ^ mask) for source in range(lax.axis_size(axis))]
    return lax.ppermute(value, axis, pairs)


def flip_blocks(values, bit_no):
    row_count, block_count, block_cols = values.shape
    span = 2**bit_no
    grouped = values.reshape(row_count, block_count // (2 * span), 2, span, block_cols)
    return jnp.flip(grouped, 2).reshape(row_count, block_count, block_cols)


def act_partner(values, bit_no, local_bits):
    if bit_no < local_bits:
        return flip_blocks(values, bit_no)
    return partner_2(values, "feat", bit_no - local_bits)


def grad_partner(values, bit_no, local_bits):
    if bit_no < local_bits:
        return flip_blocks(values, bit_no)
    return partner_2(values, "feat", bit_no - local_bits)


def gelu_exact(pre_act):
    return 0.5 * pre_act * (1.0 + lax.erf(pre_act * 0.7071067811865476))


def gelu_slope(pre_act):
    return (
        0.5 * (1.0 + lax.erf(pre_act * 0.7071067811865476))
        + pre_act * jnp.exp(-0.5 * pre_act * pre_act) * 0.3989422804014327
    )


def apply_level(values, partner, factor):
    own_term = jnp.einsum("tjr,jrc->tjc", values, factor[:, 0], preferred_element_type=jnp.float32)
    other_term = jnp.einsum(
        "tjr,jrc->tjc", partner, factor[:, 1], preferred_element_type=jnp.float32
    )
    return own_term + other_term


def gather_level(factor_shard):
    return lax.all_gather(factor_shard, "dp", axis=2, tiled=True)


def sum_level(level_grad):
    return lax.psum_scatter(
        level_grad.astype(jnp.bfloat16), "dp", scatter_dimension=2, tiled=True
    ).astype(jnp.float32)


def forward_map(current, factors, local_bits, last_plain):
    stored = []
    for layer_no in range(len(factors)):
        partner = act_partner(current, layer_no, local_bits)
        stored.append((current, partner))
        summed = apply_level(current, partner, factors[layer_no])
        if layer_no < len(factors) - 1 or not last_plain:
            current = summed.astype(jnp.bfloat16)
    return (summed, current, stored)


def backward_map(grad_in, stored, factors, local_bits, grad_scale):
    level_grads = [None] * len(factors)
    current = grad_in
    for layer_no in reversed(range(len(factors))):
        values, partner = stored[layer_no]
        factor = factors[layer_no]
        d_self = jnp.einsum("tjr,tjc->jrc", values, current, preferred_element_type=jnp.float32)
        d_part = jnp.einsum("tjr,tjc->jrc", partner, current, preferred_element_type=jnp.float32)
        level_grad = jnp.stack([d_self, d_part], 1) * grad_scale
        level_grads[layer_no] = sum_level(level_grad)
        outgoing = jnp.einsum(
            "tjc,jrc->tjr", current, factor[:, 1], preferred_element_type=jnp.float32
        ).astype(jnp.bfloat16)
        incoming = grad_partner(outgoing, layer_no, local_bits)
        own_term = jnp.einsum(
            "tjc,jrc->tjr", current, factor[:, 0], preferred_element_type=jnp.float32
        )
        current = (own_term + incoming.astype(jnp.float32)).astype(jnp.bfloat16)
    stacked = jnp.stack(level_grads, 0)
    return (current, stacked)


def on_device(tokens, cotangent, factor_in, factor_out):
    level_count = factor_in.shape[0]
    block_cols = factor_in.shape[4]
    local_blocks = factor_in.shape[1]
    local_bits = local_blocks.bit_length() - 1
    tok_rows = tokens.shape[0]
    grad_scale = 1.0 / math.sqrt(tok_rows * lax.axis_size("dp"))
    factors_first = [gather_level(factor_in[layer_no]) for layer_no in range(level_count)]
    factors_second = [gather_level(factor_out[layer_no]) for layer_no in range(level_count)]
    current = tokens.reshape(tok_rows, local_blocks, block_cols)
    pre_gelu, unused_last, stored_in = forward_map(current, factors_first, local_bits, True)
    hidden = gelu_exact(pre_gelu).astype(jnp.bfloat16)
    unused_sum, mapped, stored_out = forward_map(hidden, factors_second, local_bits, False)
    outputs = mapped.reshape(tok_rows, local_blocks * block_cols)
    grad_mid, factor_out_grad = backward_map(
        cotangent.reshape(tok_rows, local_blocks, block_cols),
        stored_out,
        factors_second,
        local_bits,
        grad_scale,
    )
    grad_pre = (grad_mid.astype(jnp.float32) * gelu_slope(pre_gelu)).astype(jnp.bfloat16)
    token_grad, factor_in_grad = backward_map(
        grad_pre, stored_in, factors_first, local_bits, grad_scale
    )
    return (
        outputs,
        token_grad.reshape(tok_rows, local_blocks * block_cols),
        factor_in_grad,
        factor_out_grad,
    )


def block_of(values, j, width):
    return values[:, j * width:(j + 1) * width]


def start_factor_copies(pieces, factor_buf, sems, levels):
    me = lax.axis_index("dp")
    rows = pieces[0].shape[3]
    copies = []
    for slot, level in enumerate(levels):
        row = []
        for k, piece in enumerate(pieces):
            at = pl.multiple_of((me ^ k) * rows, rows)
            copy = pltpu.make_async_copy(
                piece.at[level],
                factor_buf.at[slot, :, :, pl.ds(at, rows), :],
                sems.at[slot, k],
            )
            copy.start()
            row.append(copy)
        copies.append(row)
    return copies


def merged(factor_buf, slot, j):
    both = factor_buf[slot, j]
    return both.reshape(both.shape[0] * both.shape[1], both.shape[2])


def forward_kernel(levels, bits, partner_given, *refs):
    n = len(levels)
    values = refs[0]
    partner = refs[1] if partner_given else None
    base = 2 if partner_given else 1
    pieces = refs[base:base + 4]
    outs = refs[base + 4:base + 4 + n]
    factor_buf, sems = refs[base + 4 + n:]
    width = factor_buf.shape[3]
    count = factor_buf.shape[1]
    copies = start_factor_copies(pieces, factor_buf, sems, levels)
    for slot in range(n):
        for copy in copies[slot]:
            copy.wait()
        for j in range(count):
            if partner_given:
                other = block_of(partner, j, width)
            else:
                other = block_of(values, j ^ (1 << bits[slot]), width)
            pair = jnp.concatenate([block_of(values, j, width), other], axis=1)
            got = jnp.dot(pair, merged(factor_buf, slot, j), preferred_element_type=jnp.float32)
            outs[slot][:, j * width:(j + 1) * width] = got.astype(outs[slot].dtype)
        values = outs[slot]


def backward_kernel(levels, bits, remote, summed, *refs):
    n = len(levels)
    base = 2 if summed else 1
    pieces = refs[base:base + 4]
    n_out = (2 if remote else n) + (1 if summed else 0)
    outs = list(refs[base + 4:base + 4 + n_out])
    factor_buf, sems = refs[base + 4 + n_out:base + 6 + n_out]
    width = factor_buf.shape[3]
    count = factor_buf.shape[1]
    copies = start_factor_copies(pieces, factor_buf, sems, levels)
    current = refs[0]
    if summed:
        first = outs.pop(0)
        first[...] = (refs[0][...] + refs[1][...].astype(jnp.float32)).astype(first.dtype)
        current = first
    for slot in range(n):
        for copy in copies[slot]:
            copy.wait()

        def through(j):
            got = lax.dot_general(
                block_of(current, j, width),
                merged(factor_buf, slot, j),
                (((1,), (1,)), ((), ())),
                preferred_element_type=jnp.float32,
            )
            return got[:, :width], got[:, width:].astype(jnp.bfloat16)

        for j in range(count):
            if remote:
                own, other = through(j)
                outs[0][:, j * width:(j + 1) * width] = own
                outs[1][:, j * width:(j + 1) * width] = other
            else:
                p = j ^ (1 << bits[slot])
                if p < j:
                    continue
                own_j, other_j = through(j)
                own_p, other_p = through(p)
                dst = outs[slot]
                dst[:, j * width:(j + 1) * width] = (
                    own_j + other_p.astype(jnp.float32)
                ).astype(dst.dtype)
                dst[:, p * width:(p + 1) * width] = (
                    own_p + other_j.astype(jnp.float32)
                ).astype(dst.dtype)
        if not remote:
            current = outs[slot]


def grad_kernel(bits, remote, grad_scale, *refs):
    n = len(bits)
    values = refs[:n]
    partners = refs[n:2 * n] if remote else None
    base = 2 * n if remote else n
    grads = refs[base:base + n]
    keep, send = refs[base + n:]
    count = keep.shape[2]
    rows = keep.shape[4]
    width = keep.shape[5]
    me = lax.axis_index("dp")
    core = me % 2
    x_at = me // 2
    for slot in range(n):
        for j in range(count):
            if remote:
                other = block_of(partners[slot], j, width)
            else:
                other = block_of(values[slot], j ^ (1 << bits[slot]), width)
            pair = jnp.concatenate([block_of(values[slot], j, width), other], axis=1)
            got = lax.dot_general(
                pair,
                block_of(grads[slot], j, width),
                (((0,), (0,)), ((), ())),
                preferred_element_type=jnp.float32,
            ) * grad_scale
            for term in range(2):
                for x_to in range(2):
                    at = term * width + x_to * 2 * rows
                    low = got[at:at + rows]
                    high = got[at + rows:at + 2 * rows]
                    k_x = x_at ^ x_to
                    keep[k_x, slot, j, term] = jnp.where(core == 0, low, high).astype(keep.dtype)
                    send[k_x, slot, j, term] = jnp.where(core == 0, high, low).astype(send.dtype)


VMEM = pl.BlockSpec(memory_space=pltpu.VMEM)
ANY = pl.BlockSpec(memory_space=pl.ANY)
PARAMS = dict(compiler_params=pltpu.CompilerParams(vmem_limit_bytes=40 * 2**20))


COST = pl.CostEstimate(flops=1, bytes_accessed=1, transcendentals=0)


def call_forward(values, partner, pieces, levels, bits, out_type=jnp.bfloat16):
    n = len(levels)
    _, count, two, rows, width = pieces[0].shape
    acts = [values] if partner is None else [values, partner]
    buf = (n, count, two, 4 * rows, width)
    return pl.pallas_call(
        functools.partial(forward_kernel, levels, bits, partner is not None),
        out_shape=[jax.ShapeDtypeStruct(values.shape, out_type)] * n,
        in_specs=[VMEM] * len(acts) + [ANY] * 4,
        out_specs=[VMEM] * n,
        scratch_shapes=[pltpu.VMEM(buf, jnp.bfloat16), pltpu.SemaphoreType.DMA((n, 4))],
        cost_estimate=COST,
        **PARAMS,
    )(*acts, *pieces)


def call_backward(incoming, pieces, levels, bits, remote):
    n = len(levels)
    _, count, two, rows, width = pieces[0].shape
    buf = (n, count, two, 4 * rows, width)
    shape = incoming[0].shape
    low = jax.ShapeDtypeStruct(shape, jnp.bfloat16)
    outs = [low] if len(incoming) == 2 else []
    outs += [jax.ShapeDtypeStruct(shape, jnp.float32), low] if remote else [low] * n
    return pl.pallas_call(
        functools.partial(backward_kernel, levels, bits, remote, len(incoming) == 2),
        out_shape=outs,
        in_specs=[VMEM] * len(incoming) + [ANY] * 4,
        out_specs=[VMEM] * len(outs),
        scratch_shapes=[pltpu.VMEM(buf, jnp.bfloat16), pltpu.SemaphoreType.DMA((n, 4))],
        cost_estimate=COST,
        **PARAMS,
    )(*incoming, *pieces)


def call_grads(values, partners, grads, bits, rows, grad_scale):
    n = len(bits)
    tok_rows, features = values[0].shape
    width = 4 * rows
    count = features // width
    out = jax.ShapeDtypeStruct((2, n, count, 2, rows, width), jnp.bfloat16)
    acts = list(values) + list(partners or []) + list(grads)
    return pl.pallas_call(
        functools.partial(grad_kernel, bits, partners is not None, grad_scale),
        out_shape=[out, out],
        in_specs=[VMEM] * len(acts),
        out_specs=[VMEM] * 2,
        cost_estimate=COST,
        **PARAMS,
    )(*acts)


def partner_dp(value, mask):
    return lax.ppermute(value, "dp", [(k, k ^ mask) for k in range(lax.axis_size("dp"))])


def after(value, earlier):
    return lax.optimization_barrier((value, earlier))[0]


def gather_pairs(shard, earlier=None, between=None):
    if earlier is not None:
        shard = after(shard, earlier)
    far = partner_dp(shard, 2)
    near = partner_dp(shard, 1)
    if between is not None:
        far = after(far, between)
    return [shard, near, far, partner_dp(far, 1)]


def on_device_pairs(tokens, cotangent, factor_in, factor_out):
    level_count, local_blocks, _, rows, width = factor_in.shape
    local_bits = local_blocks.bit_length() - 1
    top = level_count - 1
    grad_scale = 1.0 / math.sqrt(tokens.shape[0] * lax.axis_size("dp"))
    low = tuple(range(local_bits))
    down = tuple(reversed(low))
    high = tuple(range(local_bits, level_count))

    out_top = gather_pairs(factor_out[top:])
    in_low = gather_pairs(factor_in[:local_bits], out_top[2])
    gathered = {}

    def over_feat(value, level):
        return partner_2(value, "feat", level - local_bits)

    def in_place(level):
        return gathered["in_high"], level - local_bits

    def out_place(level):
        return (out_top, 0) if level == top else (gathered["out_high"], level - local_bits)

    def forward_low(values, pieces):
        return [values] + list(call_forward(values, None, pieces, low, low))

    def forward_high(value, partner, place, level, out_type=jnp.bfloat16):
        pieces, at = place(level)
        return call_forward(value, partner, pieces, (at,), (level,), out_type)[0]

    def backward_high(incoming, place, level):
        pieces, at = place(level)
        *head, own, other = call_backward(incoming, pieces, (at,), (level,), True)
        return (head[0] if head else incoming[0]), [own, over_feat(other, level)]

    def start_sums(values, partners, grads, group):
        remote = group[0] >= local_bits
        keep, send = call_grads(
            [values[level] for level in group],
            [partners[level] for level in group] if remote else None,
            [grads[level] for level in group],
            group,
            rows,
            grad_scale,
        )
        got = partner_dp(send, 1)
        across = (keep[1].astype(jnp.float32) + got[1].astype(jnp.float32)).astype(jnp.bfloat16)
        mine = keep[0].astype(jnp.float32) + got[0].astype(jnp.float32)
        return across, mine

    def cross(started):
        across, mine = started
        return partner_dp(across, 2), mine

    def end_sums(crossed):
        far, mine = crossed
        return mine + far.astype(jnp.float32)

    grads_out, partners_in = {}, {}
    incoming = [cotangent]
    grads_out[top], incoming = backward_high(incoming, out_place, top)
    gathered["in_high"] = gather_pairs(factor_in[local_bits:], (in_low[2], incoming[0]))
    acts_in = forward_low(tokens, in_low)
    gathered["out_high"] = gather_pairs(
        factor_out[local_bits:top], (gathered["in_high"][2], acts_in[-1], incoming[1])
    )
    for level in high:
        partners_in[level] = over_feat(acts_in[level], level)
        out_type = jnp.float32 if level == top else jnp.bfloat16
        acts_in.append(forward_high(acts_in[level], partners_in[level], in_place, level, out_type))
    out_low = gather_pairs(
        factor_out[:local_bits], (gathered["out_high"][2], acts_in[local_bits + 1]), acts_in[top]
    )
    for level in reversed(high[:-1]):
        grads_out[level], incoming = backward_high(incoming, out_place, level)
    got = call_backward(incoming, out_low, down, down, False)
    for place, level in enumerate(down):
        grads_out[level] = got[place]
    grad_mid, pre_gelu = got[-1], acts_in[-1]
    hidden = gelu_exact(pre_gelu).astype(jnp.bfloat16)
    grad_pre = (grad_mid.astype(jnp.float32) * gelu_slope(pre_gelu)).astype(jnp.bfloat16)

    grads_in, partners_out, sums_in, sums_out = {}, {}, {}, {}
    grads_in[top], incoming = backward_high([grad_pre], in_place, top)
    acts_out = forward_low(hidden, out_low)
    sums_in[top] = start_sums(acts_in, partners_in, grads_in, (top,))
    sums_out[0] = start_sums(acts_out, partners_out, grads_out, low)
    for level in high:
        partners_out[level] = over_feat(acts_out[level], level)
        if level == local_bits:
            partners_out[level] = after(
                partners_out[level], (incoming[1], sums_in[top][0], sums_out[0][0])
            )
        acts_out.append(forward_high(acts_out[level], partners_out[level], out_place, level))
    middle = high[:-1]
    for level in reversed(middle):
        if level == top - 1:
            incoming[0] = after(incoming[0], (sums_in[top][0], sums_out[0][0]))
        if level == local_bits:
            sums_in[top], sums_out[0] = cross(sums_in[top]), cross(sums_out[0])
            sums_out[local_bits] = start_sums(acts_out, partners_out, grads_out, middle)
            ready = (acts_out[top], sums_in[top][0], sums_out[0][0])
            incoming[0] = after(incoming[0], ready)
        grads_in[level], incoming = backward_high(incoming, in_place, level)
    sums_in[local_bits] = start_sums(acts_in, partners_in, grads_in, middle)
    sums_out[local_bits] = cross(sums_out[local_bits])
    ready = (sums_in[local_bits][0], partners_out[top])
    incoming[0] = after(incoming[0], ready)
    got = call_backward(incoming, in_low, down, down, False)
    for place, level in enumerate(down):
        grads_in[level] = got[place]
    sums_in[local_bits] = cross(sums_in[local_bits])
    sums_out[top] = cross(start_sums(acts_out, partners_out, grads_out, (top,)))
    across, mine = start_sums(acts_in, partners_in, grads_in, low)
    sums_in[0] = cross((after(across, sums_in[local_bits][0]), mine))
    return (
        acts_out[-1],
        got[-1],
        jnp.concatenate([end_sums(sums_in[level]) for level in sorted(sums_in)], 0),
        jnp.concatenate([end_sums(sums_out[level]) for level in sorted(sums_out)], 0),
    )


def solution(mesh):
    placed = (
        P("dp", "feat"),
        P("dp", "feat"),
        P(None, "feat", None, "dp", None),
        P(None, "feat", None, "dp", None),
    )
    pairs = mesh.shape["dp"] == 4
    return jax.shard_map(
        on_device_pairs if pairs else on_device,
        mesh=mesh,
        in_specs=placed,
        out_specs=(
            P("dp", "feat"),
            P("dp", "feat"),
            P(None, "feat", None, "dp", None),
            P(None, "feat", None, "dp", None),
        ),
        check_vma=False,
    )
```
